32 devices in a mesh: seq: 4 (over z), exp: 4 (over y, x), edp: 2 (over core).
Axes of the slice: x: 2, y: 2, z: 4, core: 2. Of those that a mesh axis runs over, the one named last changes fastest.
Arguments:
- tokens: bfloat16 [4096, 2048], P(('seq', 'exp', 'edp')), may hold values from -6 to 6
- route_ids: int32 [4096, 8], P(('seq', 'exp', 'edp')), may hold values from 0 to 15, all different within a row; in each aligned block of 128 rows (0 to 127, 128 to 255, ...) at most 72 rows name the same one
- gates: float32 [4096, 8], P(('seq', 'exp', 'edp')), may hold values from 0.05 to 0.5
- d_out: bfloat16 [4096, 2048], P(('seq', 'exp', 'edp')), may hold values from -6 to 6
- w_gate: bfloat16 [16, 2048, 384], P(('seq', 'exp')), may hold values from -0.125 to 0.125
- w_up: bfloat16 [16, 2048, 384], P(('seq', 'exp')), may hold values from -0.125 to 0.125
- w_down: bfloat16 [16, 2048, 384], P(('seq', 'exp')), may hold values from -0.3125 to 0.3125
Outputs:
- d_tokens: bfloat16 [4096, 2048], P(('seq', 'exp', 'edp'))
- grad_gate: float32 [16, 2048, 384], P(('seq', 'exp'), 'edp')
- grad_up: float32 [16, 2048, 384], P(('seq', 'exp'), 'edp')
- grad_down: float32 [16, 2048, 384], P(('seq', 'exp'), 'edp')
The draws below stay inside these ranges and needn't reach their ends.
Inputs may be any that keep to these rules, and one draw needn't show every extreme that they name: `route_ids`: among the 128 tokens of one device no expert is named more than 72 times, a bound that some block reaches; a token names 8 different experts.
All inputs are finite; a program needn't handle non-finite values.
Results may differ from the reference program's by a relative error of at most 0.0064.
Values may be sent and summed in bfloat16 or wider, within the bound.
A program may use at most 128 MiB of HBM per device.

```python
import math
import jax
import jax.numpy as jnp
import numpy as np
from jax import lax

D = 2048
HID = 384
TOPK = 8
TOK_DEV = 128
EXPERTS = 16
CAP = 72
TOKENS = 4096
N_SEQ = 4
N_EXP = 4
N_EDP = 2


def level_of(rng, extent, pieces, low, high):
    def one(axis_at, parts):
        heights = jax.random.uniform(jax.random.fold_in(jax.random.fold_in(rng, 6), axis_at), (parts,), jnp.float32, low / len(pieces), high / len(pieces))
        return jnp.repeat(jnp.exp(heights), extent[axis_at] // parts).reshape((-1,) + (1,) * (len(extent) - axis_at - 1))

    level = one(*pieces[0])
    for cut in pieces[1:]:
        level = level * one(*cut)
    return level


def deal_out(own_key, own, number, rows, count, top, bound, skew):
    ranking = jax.random.permutation(own_key, count)
    crowded, usual = load_shares(count, rows * top, bound, skew, True), load_shares(count, rows * top, bound, skew, False)
    places = jnp.arange(count)

    def named(lengths, rotation):
        used = int((lengths > 0).sum())
        fixed = max(1, used // 4)
        shifted = fixed + (places - fixed + rotation * (used - fixed)) % max(1, count - fixed)
        return jnp.zeros((count,), jnp.int32).at[ranking[jnp.where(places < fixed, places, shifted)]].set(jnp.asarray(lengths, jnp.int32))

    lengths = jnp.where(number % 4 == 0, named(crowded, number // 4), named(usual, number - number // 4 - 1))
    mixed = jax.random.permutation(jax.random.fold_in(own, 3), count)
    source_of, sink = mixed[0:count // 2 * 2:2], mixed[1:count // 2 * 2:2]
    slack = jnp.minimum(lengths[source_of] - 1, bound - lengths[sink]) // 2
    slack = jnp.where((source_of == ranking[0]) | (sink == ranking[0]) | (lengths[sink] == 0), 0, jnp.maximum(slack, 0))
    shifted = jax.random.randint(jax.random.fold_in(own, 4), (count // 2,), 0, 1 << 20) % (slack + 1)
    lengths = lengths.at[source_of].add(-shifted).at[sink].add(shifted)
    labels = jnp.searchsorted(jnp.cumsum(lengths), jnp.arange(rows * top), side="right").astype(jnp.int32)
    listing = labels.reshape(top, rows).T
    listing = listing[jax.random.permutation(jax.random.fold_in(own, 1), rows)]
    rotation = jax.random.randint(jax.random.fold_in(own, 2), (rows, 1), 0, top)
    return jnp.take_along_axis(listing, (jnp.arange(top)[None, :] + rotation) % top, axis=1)


def load_shares(number_of, total, bound, slope, full):
    portions = [(1 << 20) // math.isqrt(rank ** slope) + 1 for rank in range(1, number_of + 1)]
    largest = bound if full else min(bound, max(-(-total // number_of), total * portions[0] // sum(portions)))
    least = 1 if total - largest >= number_of - 1 else 0
    holding, surplus = [largest] + [least] * (number_of - 1), total - largest - least * (number_of - 1)
    while surplus > 0:
        candidates = [i for i in range(1, number_of) if holding[i] < largest] or [i for i in range(1, number_of) if holding[i] < bound]
        pool, left = sum([portions[i] for i in candidates]), surplus
        for i in candidates:
            extra = min(bound - holding[i], max(1, left * portions[i] // pool), surplus)
            holding[i] = holding[i] + extra
            surplus = surplus - extra
    return np.array(holding)


def scatter_about(own_key, dims, scale, reach, cuts=(), kind=jnp.bfloat16):
    gain = level_of(own_key, dims, cuts, -0.22, 0.18) if cuts else 1.0
    array = jax.random.normal(own_key, dims, jnp.float32) * scale * gain
    return jnp.minimum(jnp.maximum(array, -reach), reach).astype(kind)


def setup_inputs(seed: int = 0) -> dict:
    streams_of = jax.random.split(jax.random.key(seed), 8)
    tokens = scatter_about(streams_of[0], (TOKENS, D), 1.0, 6.0, ((0, 32),))
    route_ids_keys = jax.random.split(jax.random.fold_in(streams_of[1], 1), TOKENS // TOK_DEV)
    route_ids_turns = jax.random.permutation(jax.random.fold_in(streams_of[1], 3), TOKENS // TOK_DEV)
    route_ids = jax.vmap(lambda own, number: deal_out(jax.random.fold_in(streams_of[1], 2), own, number, TOK_DEV, EXPERTS, TOPK, CAP, 1))(route_ids_keys, route_ids_turns).reshape((TOKENS, TOPK))
    gates = jnp.clip(jnp.exp(math.log(0.5) - 2.3025851 * jax.random.uniform(streams_of[2], (TOKENS, TOPK), jnp.float32) ** level_of(streams_of[2], (TOKENS, TOPK), ((0, 32),), -0.2, 0.2)), 0.05, 0.5)
    d_out = scatter_about(streams_of[3], (TOKENS, D), 1.0, 6.0, ((0, 32),))
    w_gate = scatter_about(streams_of[4], (EXPERTS, D, HID), D ** -0.5, 0.125, ((0, 16),))
    w_up = scatter_about(streams_of[5], (EXPERTS, D, HID), D ** -0.5, 0.125, ((0, 16),))
    w_down = scatter_about(streams_of[6], (EXPERTS, D, HID), HID ** -0.5, 0.3125, ((0, 16),))
    return dict(tokens=tokens, route_ids=route_ids, gates=gates, d_out=d_out, w_gate=w_gate, w_up=w_up, w_down=w_down)


def expert_grads(x_rows, dy_rows, wg, wu, wd):
    a = jnp.dot(x_rows, wg, preferred_element_type=jnp.float32)
    b = jnp.dot(x_rows, wu, preferred_element_type=jnp.float32)
    sig = jax.nn.sigmoid(a)
    act = a * sig
    hidden = (act * b).astype(jnp.bfloat16)
    d_hidden = jnp.dot(dy_rows, wd, preferred_element_type=jnp.float32)
    d_gate = (d_hidden * b * sig * (1.0 + a * (1.0 - sig))).astype(jnp.bfloat16)
    d_upper = (d_hidden * act).astype(jnp.bfloat16)
    contract_one = (((1,), (1,)), ((), ()))
    contract_zero = (((0,), (0,)), ((), ()))
    back = lax.dot_general(d_gate, wg, contract_one, preferred_element_type=jnp.float32)
    back = back + lax.dot_general(d_upper, wu, contract_one, preferred_element_type=jnp.float32)
    grad_g = lax.dot_general(x_rows, d_gate, contract_zero, preferred_element_type=jnp.float32)
    grad_u = lax.dot_general(x_rows, d_upper, contract_zero, preferred_element_type=jnp.float32)
    grad_d = lax.dot_general(dy_rows, hidden, contract_zero, preferred_element_type=jnp.float32)
    return back.astype(jnp.bfloat16), grad_g, grad_u, grad_d


def reference(tokens, route_ids, gates, d_out, w_gate, w_up, w_down):
    topk = route_ids.shape[1]
    most = N_SEQ * N_EXP * N_EDP * CAP
    flat_ids = route_ids.reshape(-1)
    flat_gates = gates.reshape(-1)

    def per_expert(carry, expert):
        chosen = flat_ids == expert
        where_rows = jnp.nonzero(chosen, size=most, fill_value=0)[0].astype(jnp.int32)
        count = jnp.sum(chosen.astype(jnp.int32))
        valid = (jnp.arange(most, dtype=jnp.int32) < count)[:, None]
        owner = (where_rows // topk).astype(jnp.int32)
        x_rows = jnp.where(valid, tokens[owner], 0.0).astype(jnp.bfloat16)
        scaled = flat_gates[where_rows][:, None] * d_out[owner].astype(jnp.float32)
        dy_rows = jnp.where(valid, scaled, 0.0).astype(jnp.bfloat16)
        back, grad_g, grad_u, grad_d = expert_grads(x_rows, dy_rows, w_gate[expert], w_up[expert], w_down[expert])
        carry = carry.at[owner].add(jnp.where(valid, back.astype(jnp.float32), 0.0))
        return carry, (grad_g, grad_u, grad_d)

    start = jnp.zeros((tokens.shape[0], tokens.shape[1]), jnp.float32)
    total, grads = lax.scan(per_expert, start, jnp.arange(EXPERTS, dtype=jnp.int32))
    return total.astype(jnp.bfloat16), grads[0], grads[1], grads[2]
```

```python
import functools
import jax
import jax.numpy as jnp
from jax import lax
from jax.experimental import pallas as pl
from jax.experimental.pallas import tpu as pltpu
from jax.sharding import PartitionSpec as P

MESH = pl.DeviceIdType.MESH
BF = jnp.bfloat16
F32 = jnp.float32
VMEM_BYTES = 62 * 1024 * 1024


def expert_grads(x_rows, dy_rows, wg, wu, wd):
    a = jnp.dot(x_rows, wg, preferred_element_type=jnp.float32)
    b = jnp.dot(x_rows, wu, preferred_element_type=jnp.float32)
    sig = jax.nn.sigmoid(a)
    act = a * sig
    hidden = (act * b).astype(jnp.bfloat16)
    d_hidden = jnp.dot(dy_rows, wd, preferred_element_type=jnp.float32)
    d_gate = (d_hidden * b * sig * (1.0 + a * (1.0 - sig))).astype(jnp.bfloat16)
    d_upper = (d_hidden * act).astype(jnp.bfloat16)
    contract_one = (((1,), (1,)), ((), ()))
    contract_zero = (((0,), (0,)), ((), ()))
    back = lax.dot_general(d_gate, wg, contract_one, preferred_element_type=jnp.float32)
    back = back + lax.dot_general(d_upper, wu, contract_one, preferred_element_type=jnp.float32)
    grad_g = lax.dot_general(x_rows, d_gate, contract_zero, preferred_element_type=jnp.float32)
    grad_u = lax.dot_general(x_rows, d_upper, contract_zero, preferred_element_type=jnp.float32)
    grad_d = lax.dot_general(dy_rows, hidden, contract_zero, preferred_element_type=jnp.float32)
    return (back.astype(jnp.bfloat16), grad_g, grad_u, grad_d)


def on_device(tokens, route_ids, gates, d_out, w_gate, w_up, w_down):
    tok_count = tokens.shape[0]
    width = tokens.shape[1]
    topk = route_ids.shape[1]
    seq_count = lax.axis_size("seq")
    exp_count = lax.axis_size("exp")
    experts = seq_count * exp_count
    pairs = tok_count * topk
    capacity = pairs // experts + max(1, pairs // (8 * experts))
    flat_ids = route_ids.reshape(-1)
    onehot = (flat_ids[:, None] == jnp.arange(experts, dtype=jnp.int32)[None, :]).astype(jnp.int32)
    order = jnp.arange(pairs, dtype=jnp.int32)
    lower = (order[:, None] > order[None, :]).astype(BF)
    earlier = jnp.dot(lower, onehot.astype(BF), preferred_element_type=F32).astype(jnp.int32)
    slot_index = jnp.sum(earlier * onehot, axis=1)
    target = flat_ids * capacity + slot_index
    rows_x = jnp.broadcast_to(tokens[:, None, :], (tok_count, topk, width)).reshape(pairs, width)
    scaled = (
        (gates[:, :, None] * d_out[:, None, :].astype(jnp.float32))
        .astype(jnp.bfloat16)
        .reshape(pairs, width)
    )
    send_x = jnp.zeros((experts * capacity, width), jnp.bfloat16).at[target].set(rows_x)
    send_dy = jnp.zeros((experts * capacity, width), jnp.bfloat16).at[target].set(scaled)
    shaped = (experts, capacity, width)
    recv_x, recv_dy = (
        lax.all_to_all(
            send_x.reshape(shaped), ("seq", "exp"), split_axis=0, concat_axis=0, tiled=True
        ),
        lax.all_to_all(
            send_dy.reshape(shaped), ("seq", "exp"), split_axis=0, concat_axis=0, tiled=True
        ),
    )
    back, grad_g, grad_u, grad_d = expert_grads(
        recv_x.reshape(experts * capacity, width),
        recv_dy.reshape(experts * capacity, width),
        w_gate[0],
        w_up[0],
        w_down[0],
    )
    returned = lax.all_to_all(
        back.reshape(experts, capacity, width),
        ("seq", "exp"),
        split_axis=0,
        concat_axis=0,
        tiled=True,
    )
    returned = returned.reshape(experts * capacity, width)
    gathered = returned[target].reshape(tok_count, topk, width).astype(jnp.float32)
    d_tokens = jnp.sum(gathered, axis=1).astype(jnp.bfloat16)
    sum_g, sum_u, sum_d = (
        lax.psum_scatter(grad_g, "edp", scatter_dimension=0, tiled=True),
        lax.psum_scatter(grad_u, "edp", scatter_dimension=0, tiled=True),
        lax.psum_scatter(grad_d, "edp", scatter_dimension=0, tiled=True),
    )
    return (d_tokens, sum_g[None], sum_u[None], sum_d[None])


def fused_kernel(
    ns, ne, rows_half,
    idt_ref, gt_ref, x_ref, d_ref, wg_hbm, wu_hbm, wd_hbm,
    dt_ref, gg_ref, gu_ref, gd_ref,
    meta_o, meta_i, xin, din, pall, gcol, cx, cd, rx, rd, wgu, wd,
    ab, dh, dd, hid, bi, acc, po, pi, go, gi,
    w_sem, zs, zr, es, er, bs, br, ps, pr, gs, gr,
):
    s = lax.axis_index("seq")
    e = lax.axis_index("exp")
    c = lax.axis_index("edp")
    tok, width = x_ref.shape
    hidn = wd.shape[1]
    half_w = width // 2
    topk = idt_ref.shape[0]
    nch = ns // 2
    rows = 2 * rows_half
    allr = ne * rows
    ct = min(512, width)

    def plane(d):
        return (lax.rem(s + d, ns), e, c)

    def plane_back(d):
        return (lax.rem(s + ns - d, ns), e, c)

    def peer(j):
        return (s, lax.rem(e + j, ne), c)

    def peer_back(j):
        return (s, lax.rem(e + ne - j, ne), c)

    weights = [
        pltpu.make_async_copy(wg_hbm, wgu.at[:, 0:hidn], w_sem.at[0]),
        pltpu.make_async_copy(wu_hbm, wgu.at[:, hidn:2 * hidn], w_sem.at[1]),
        pltpu.make_async_copy(wd_hbm, wd, w_sem.at[2]),
    ]
    for w in weights:
        w.start()

    barrier = pltpu.get_barrier_semaphore()
    for d in range(1, ns):
        pl.semaphore_signal(barrier, inc=1, device_id=plane(d), device_id_type=MESH)
    for j in range(1, ne):
        pl.semaphore_signal(barrier, inc=1, device_id=peer(j), device_id_type=MESH)
    pl.semaphore_signal(barrier, inc=1, device_id=(s, e, 1 - c), device_id_type=MESH)

    experts = ns * ne
    ex = lax.broadcasted_iota(jnp.int32, (experts, tok), 0)
    mask = jnp.zeros((experts, tok), F32)
    gate = jnp.zeros((experts, tok), F32)
    for k in range(topk):
        eq = idt_ref[k:k + 1, :] == ex
        mask = jnp.where(eq, 1.0, mask)
        gate = jnp.where(eq, gt_ref[k:k + 1, :], gate)
    before = (
        lax.broadcasted_iota(jnp.int32, (tok, tok), 0)
        < lax.broadcasted_iota(jnp.int32, (tok, tok), 1)
    )
    rank = jnp.dot(
        mask.astype(BF), jnp.where(before, 1.0, 0.0).astype(BF), preferred_element_type=F32
    )
    slot = jnp.where(mask > 0.0, rank, -4096.0)
    for z in range(ns):
        meta_o[z, 0:ne, :] = slot[z * ne:(z + 1) * ne, :]
        meta_o[z, ne:2 * ne, :] = gate[z * ne:(z + 1) * ne, :]
    meta_i[0] = meta_o[s]

    pl.semaphore_wait(barrier, ns - 1 + ne - 1 + 1)

    def remote(src, dst, ss, rs, dev):
        return pltpu.make_async_remote_copy(
            src_ref=src, dst_ref=dst, send_sem=ss, recv_sem=rs, device_id=dev, device_id_type=MESH
        )

    mcp = [None] * ns
    xcp = [None] * ns
    dcp = [None] * ns
    for d in range(1, ns):
        mcp[d] = remote(
            meta_o.at[lax.rem(s + d, ns)], meta_i.at[d], zs.at[0, d], zr.at[0, d], plane(d)
        )
        xcp[d] = remote(x_ref, xin.at[d], zs.at[1, d], zr.at[1, d], plane(d))
        dcp[d] = remote(d_ref, din.at[d], zs.at[2, d], zr.at[2, d], plane(d))
    xout = [[None] * ne for _ in range(nch)]
    dout = [[None] * ne for _ in range(nch)]
    bout = [[None] * ne for _ in range(nch)]
    for k in range(nch):
        for j in range(1, ne):
            xout[k][j] = remote(cx.at[k, j], rx.at[k, j], es.at[0, k, j], er.at[0, k, j], peer(j))
            dout[k][j] = remote(cd.at[k, j], rd.at[k, j], es.at[1, k, j], er.at[1, k, j], peer(j))
            bout[k][j] = remote(cx.at[k, j], bi.at[k, j], bs.at[k, j], br.at[k, j], peer_back(j))
    pout = [None] * ns
    for d in range(1, ns):
        pout[d] = remote(po.at[d], pi.at[d], ps.at[d], pr.at[d], plane_back(d))
    partner = (s, e, 1 - c)
    gout = [
        remote(go.at[i], gi.at[i], gs.at[i], gr.at[i], partner) for i in range(3)
    ]

    def members(k):
        return (k, k + nch)

    def column(t, size):
        return pl.ds(pl.multiple_of(t * size, size), size)

    def make_select(k):
        da_, db_ = members(k)
        r = lax.broadcasted_iota(jnp.int32, (rows, 2 * tok), 0).astype(F32)
        for j in range(ne):
            idx = lax.rem(e + j, ne)
            sl = jnp.concatenate(
                [
                    meta_i[da_, pl.ds(idx, 1), :],
                    meta_i[db_, pl.ds(idx, 1), :] + float(rows_half),
                ],
                axis=1,
            )
            gl = jnp.concatenate(
                [meta_i[da_, pl.ds(ne + idx, 1), :], meta_i[db_, pl.ds(ne + idx, 1), :]], axis=1
            )
            hit = r == sl
            pall[k, j * rows:(j + 1) * rows, :] = jnp.where(hit, 1.0, 0.0).astype(BF)
            g = jnp.sum(jnp.where(hit, gl, 0.0), axis=1, keepdims=True)
            gcol[j * rows:(j + 1) * rows, :] = jnp.broadcast_to(g, (rows, 128))

    def compact(k, own, arrived, out, got, scaled):
        ra, rb = members(k)

        def body(t, carry):
            cs = column(t, ct)
            first = own[:, cs] if ra == 0 else arrived[ra, :, cs]
            both = jnp.concatenate([first, arrived[rb, :, cs]], axis=0)
            y = jnp.dot(pall[k], both, preferred_element_type=F32)
            if scaled:
                y = y * gcol[:, 0:1]
            y = y.astype(BF)
            got[k, 0, :, cs] = y[0:rows]
            for j in range(1, ne):
                out[k, j, :, cs] = y[j * rows:(j + 1) * rows]
            return carry

        lax.fori_loop(0, width // ct, body, 0)

    def gate_up(k):
        for j in range(1, ne):
            xout[k][j].wait_recv()

        def body(t, carry):
            cs = column(t, 256)
            ab[:, cs] = jnp.dot(
                rx[k].reshape(allr, width), wgu[:, cs], preferred_element_type=F32
            )
            return carry

        lax.fori_loop(0, 2 * hidn // 256, body, 0)

    def middle(k):
        for j in range(1, ne):
            dout[k][j].wait_recv()
        dh[...] = jnp.dot(rd[k].reshape(allr, width), wd[...], preferred_element_type=F32)

        def act_body(t, carry):
            rs_ = pl.ds(pl.multiple_of(t * 16, 16), 16)
            a = ab[rs_, 0:hidn]
            b = ab[rs_, hidn:2 * hidn]
            g = dh[rs_, :]
            sig = jax.nn.sigmoid(a)
            act = a * sig
            hid[rs_, :] = (act * b).astype(BF)
            dd[rs_, 0:hidn] = (g * b * sig * (1.0 + a * (1.0 - sig))).astype(BF)
            dd[rs_, hidn:2 * hidn] = (g * act).astype(BF)
            return carry

        lax.fori_loop(0, allr // 16, act_body, 0)
        for j in range(1, ne):
            xout[k][j].wait_send()

        def back_body(t, carry):
            cs = column(t, ct)
            y = lax.dot_general(
                dd[...], wgu[cs, :], (((1,), (1,)), ((), ())), preferred_element_type=F32
            ).astype(BF)
            bi[k, 0, :, cs] = y[0:rows]
            for j in range(1, ne):
                cx[k, j, :, cs] = y[j * rows:(j + 1) * rows]
            return carry

        lax.fori_loop(0, width // ct, back_body, 0)
        for j in range(1, ne):
            bout[k][j].start()

    zero = (((0,), (0,)), ((), ()))

    def grads(k, half, outs):
        gt = min(256, half_w)

        def body(t, carry):
            cs = pl.ds(pl.multiple_of(half * half_w + t * gt, gt), gt)
            rs_ = column(t, gt)
            xt = rx[k, :, :, cs].reshape(allr, gt)
            dt = rd[k, :, :, cs].reshape(allr, gt)
            xg = lax.dot_general(xt, dd[...], zero, preferred_element_type=F32)
            dg = lax.dot_general(dt, hid[...], zero, preferred_element_type=F32)
            if k == 0:
                outs[0][rs_, :] = xg[:, 0:hidn]
                outs[1][rs_, :] = xg[:, hidn:2 * hidn]
                outs[2][rs_, :] = dg
            else:
                outs[0][rs_, :] += xg[:, 0:hidn]
                outs[1][rs_, :] += xg[:, hidn:2 * hidn]
                outs[2][rs_, :] += dg
            return carry

        lax.fori_loop(0, half_w // gt, body, 0)

    def combine(k):
        for j in range(1, ne):
            bout[k][j].wait_recv()
        ra, rb = members(k)

        def body(t, carry):
            cs = column(t, ct)
            y = lax.dot_general(
                pall[k], bi[k, :, :, cs].reshape(allr, ct), zero, preferred_element_type=F32
            )
            if ra == 0:
                acc[:, cs] = y[0:tok]
            else:
                po[ra, :, cs] = y[0:tok].astype(BF)
            po[rb, :, cs] = y[tok:2 * tok].astype(BF)
            return carry

        lax.fori_loop(0, width // ct, body, 0)
        for d in (ra, rb):
            if d:
                pout[d].start()

    def arrive(copies, k):
        for d in members(k):
            if d:
                copies[d].wait_recv()

    def depart(copies, k):
        for d in members(k):
            if d:
                copies[d].start()

    for d in range(1, ns):
        mcp[d].start()
    depart(xcp, 0)
    arrive(mcp, 0)
    make_select(0)
    for k in range(nch):
        if k:
            arrive(mcp, k)
            make_select(k)
        arrive(xcp, k)
        if k == 0:
            depart(dcp, 0)
            if nch > 1:
                depart(xcp, 1)
        compact(k, x_ref, xin, cx, rx, False)
        for j in range(1, ne):
            xout[k][j].start()
        if k:
            middle(k - 1)
        arrive(dcp, k)
        if k + 1 < nch:
            depart(dcp, k + 1)
        if k and k + 1 < nch:
            depart(xcp, k + 1)
        compact(k, d_ref, din, cd, rd, True)
        for j in range(1, ne):
            dout[k][j].start()
        if k == 0:
            for w in weights:
                w.wait()
        else:
            grads(k - 1, 1 - c, (go.at[0], go.at[1], go.at[2]))
            grads(k - 1, c, (gg_ref, gu_ref, gd_ref))
            combine(k - 1)
        gate_up(k)
    last = nch - 1
    middle(last)
    grads(last, 1 - c, (go.at[0], go.at[1], go.at[2]))
    for g in gout:
        g.start()
    grads(last, c, (gg_ref, gu_ref, gd_ref))
    combine(last)
    for g in gout:
        g.wait_recv()
    gg_ref[...] += gi[0]
    gu_ref[...] += gi[1]
    gd_ref[...] += gi[2]
    for d in range(1, ns):
        pout[d].wait_recv()

    def final(t, carry):
        cs = column(t, ct)
        y = acc[:, cs]
        for d in range(1, ns):
            y = y + pi[d, :, cs].astype(F32)
        dt_ref[:, cs] = y.astype(BF)
        return carry

    lax.fori_loop(0, width // ct, final, 0)
    for d in range(1, ns):
        mcp[d].wait_send()
        xcp[d].wait_send()
        dcp[d].wait_send()
        pout[d].wait_send()
    for k in range(nch):
        for j in range(1, ne):
            dout[k][j].wait_send()
            bout[k][j].wait_send()
    for g in gout:
        g.wait_send()


def sizes(ns, ne, tok, topk, width, hidn):
    experts = ns * ne
    capacity = tok * topk // experts + max(1, tok * topk // (8 * experts))
    rows_half = -(-capacity // 8) * 8
    rows = 2 * rows_half
    nch = max(1, ns // 2)
    allr = ne * rows
    scratch = [
        ((ns, 2 * ne, tok), F32),
        ((ns, 2 * ne, tok), F32),
        ((ns, tok, width), BF),
        ((ns, tok, width), BF),
        ((nch, allr, 2 * tok), BF),
        ((allr, 128), F32),
        ((nch, ne, rows, width), BF),
        ((nch, ne, rows, width), BF),
        ((nch, ne, rows, width), BF),
        ((nch, ne, rows, width), BF),
        ((width, 2 * hidn), BF),
        ((width, hidn), BF),
        ((allr, 2 * hidn), F32),
        ((allr, hidn), F32),
        ((allr, 2 * hidn), BF),
        ((allr, hidn), BF),
        ((nch, ne, rows, width), BF),
        ((tok, width), F32),
        ((ns, tok, width), BF),
        ((ns, tok, width), BF),
        ((3, width // 2, hidn), F32),
        ((3, width // 2, hidn), F32),
    ]
    total = 0
    for shape, kind in scratch:
        n = 1
        for v in shape:
            n *= v
        total += n * jnp.dtype(kind).itemsize
    total += 3 * (width // 2) * hidn * 4 + 3 * tok * width * 2
    return rows_half, nch, scratch, total


def fused(tokens, route_ids, gates, d_out, w_gate, w_up, w_down):
    ns = lax.axis_size("seq")
    ne = lax.axis_size("exp")
    tok, width = tokens.shape
    topk = route_ids.shape[1]
    hidn = w_gate.shape[2]
    rows_half, nch, scratch, _ = sizes(ns, ne, tok, topk, width, hidn)
    dma = pltpu.SemaphoreType.DMA
    vm = pl.BlockSpec(memory_space=pltpu.VMEM)
    hbm = pl.BlockSpec(memory_space=pl.ANY)
    half = jax.ShapeDtypeStruct((width // 2, hidn), F32)
    pairs = tok * ns * topk * 9 // 8
    out = pl.pallas_call(
        functools.partial(fused_kernel, ns, ne, rows_half),
        out_shape=(jax.ShapeDtypeStruct((tok, width), BF), half, half, half),
        in_specs=[vm, vm, vm, vm, hbm, hbm, hbm],
        out_specs=(vm, vm, vm, vm),
        scratch_shapes=[pltpu.VMEM(sh, kind) for sh, kind in scratch] + [
            dma((3,)),
            dma((3, ns)), dma((3, ns)),
            dma((2, nch, ne)), dma((2, nch, ne)),
            dma((nch, ne)), dma((nch, ne)),
            dma((ns,)), dma((ns,)),
            dma((3,)), dma((3,)),
        ],
        compiler_params=pltpu.CompilerParams(
            collective_id=0, has_side_effects=True, vmem_limit_bytes=VMEM_BYTES
        ),
        cost_estimate=pl.CostEstimate(
            flops=16 * pairs * width * hidn, bytes_accessed=12 * width * hidn, transcendentals=0
        ),
    )(route_ids.T, gates.T, tokens, d_out, w_gate[0], w_up[0], w_down[0])
    return (out[0], out[1][None], out[2][None], out[3][None])


def solution(mesh):
    in_specs = (
        P(("seq", "exp", "edp"), None),
        P(("seq", "exp", "edp"), None),
        P(("seq", "exp", "edp"), None),
        P(("seq", "exp", "edp"), None),
        P(("seq", "exp"), None, None),
        P(("seq", "exp"), None, None),
        P(("seq", "exp"), None, None),
    )
    out_specs = (
        P(("seq", "exp", "edp"), None),
        P(("seq", "exp"), "edp", None),
        P(("seq", "exp"), "edp", None),
        P(("seq", "exp"), "edp", None),
    )
    def shard(body):
        return jax.shard_map(
            body, mesh=mesh, in_specs=in_specs, out_specs=out_specs, check_vma=False
        )

    ns, ne, nd = mesh.shape["seq"], mesh.shape["exp"], mesh.shape["edp"]

    def whole(tokens, route_ids, gates, d_out, w_gate, w_up, w_down):
        tok = tokens.shape[0] // (ns * ne * nd)
        total = sizes(ns, ne, tok, route_ids.shape[1], tokens.shape[1], w_gate.shape[2])[3]
        fits = total < VMEM_BYTES - 3 * 1024 * 1024
        body = fused if fits and ns % 2 == 0 and nd == 2 and tok % 128 == 0 else on_device
        return shard(body)(tokens, route_ids, gates, d_out, w_gate, w_up, w_down)

    return whole
```

```python
import functools
import jax
import jax.numpy as jnp
from jax import lax
from jax.experimental import pallas as pl
from jax.experimental.pallas import tpu as pltpu
from jax.sharding import PartitionSpec as P

MESH = pl.DeviceIdType.MESH
BF = jnp.bfloat16
F32 = jnp.float32
VMEM_BYTES = 62 * 1024 * 1024
PARTS = 4


def expert_grads(x_rows, dy_rows, wg, wu, wd):
    a = jnp.dot(x_rows, wg, preferred_element_type=jnp.float32)
    b = jnp.dot(x_rows, wu, preferred_element_type=jnp.float32)
    sig = jax.nn.sigmoid(a)
    act = a * sig
    hidden = (act * b).astype(jnp.bfloat16)
    d_hidden = jnp.dot(dy_rows, wd, preferred_element_type=jnp.float32)
    d_gate = (d_hidden * b * sig * (1.0 + a * (1.0 - sig))).astype(jnp.bfloat16)
    d_upper = (d_hidden * act).astype(jnp.bfloat16)
    contract_one = (((1,), (1,)), ((), ()))
    contract_zero = (((0,), (0,)), ((), ()))
    back = lax.dot_general(d_gate, wg, contract_one, preferred_element_type=jnp.float32)
    back = back + lax.dot_general(d_upper, wu, contract_one, preferred_element_type=jnp.float32)
    grad_g = lax.dot_general(x_rows, d_gate, contract_zero, preferred_element_type=jnp.float32)
    grad_u = lax.dot_general(x_rows, d_upper, contract_zero, preferred_element_type=jnp.float32)
    grad_d = lax.dot_general(dy_rows, hidden, contract_zero, preferred_element_type=jnp.float32)
    return (back.astype(jnp.bfloat16), grad_g, grad_u, grad_d)


def on_device(tokens, route_ids, gates, d_out, w_gate, w_up, w_down):
    tok_count = tokens.shape[0]
    width = tokens.shape[1]
    topk = route_ids.shape[1]
    seq_count = lax.axis_size("seq")
    exp_count = lax.axis_size("exp")
    experts = seq_count * exp_count
    pairs = tok_count * topk
    capacity = pairs // experts + max(1, pairs // (8 * experts))
    flat_ids = route_ids.reshape(-1)
    onehot = (flat_ids[:, None] == jnp.arange(experts, dtype=jnp.int32)[None, :]).astype(jnp.int32)
    order = jnp.arange(pairs, dtype=jnp.int32)
    lower = (order[:, None] > order[None, :]).astype(BF)
    earlier = jnp.dot(lower, onehot.astype(BF), preferred_element_type=F32).astype(jnp.int32)
    slot_index = jnp.sum(earlier * onehot, axis=1)
    target = flat_ids * capacity + slot_index
    rows_x = jnp.broadcast_to(tokens[:, None, :], (tok_count, topk, width)).reshape(pairs, width)
    scaled = (
        (gates[:, :, None] * d_out[:, None, :].astype(jnp.float32))
        .astype(jnp.bfloat16)
        .reshape(pairs, width)
    )
    send_x = jnp.zeros((experts * capacity, width), jnp.bfloat16).at[target].set(rows_x)
    send_dy = jnp.zeros((experts * capacity, width), jnp.bfloat16).at[target].set(scaled)
    shaped = (experts, capacity, width)
    recv_x, recv_dy = (
        lax.all_to_all(
            send_x.reshape(shaped), ("seq", "exp"), split_axis=0, concat_axis=0, tiled=True
        ),
        lax.all_to_all(
            send_dy.reshape(shaped), ("seq", "exp"), split_axis=0, concat_axis=0, tiled=True
        ),
    )
    back, grad_g, grad_u, grad_d = expert_grads(
        recv_x.reshape(experts * capacity, width),
        recv_dy.reshape(experts * capacity, width),
        w_gate[0],
        w_up[0],
        w_down[0],
    )
    returned = lax.all_to_all(
        back.reshape(experts, capacity, width),
        ("seq", "exp"),
        split_axis=0,
        concat_axis=0,
        tiled=True,
    )
    returned = returned.reshape(experts * capacity, width)
    gathered = returned[target].reshape(tok_count, topk, width).astype(jnp.float32)
    d_tokens = jnp.sum(gathered, axis=1).astype(jnp.bfloat16)
    sum_g, sum_u, sum_d = (
        lax.psum_scatter(grad_g, "edp", scatter_dimension=0, tiled=True),
        lax.psum_scatter(grad_u, "edp", scatter_dimension=0, tiled=True),
        lax.psum_scatter(grad_d, "edp", scatter_dimension=0, tiled=True),
    )
    return (d_tokens, sum_g[None], sum_u[None], sum_d[None])


def far_first(ne):
    return range(ne - 1, 0, -1)


def fused_kernel(
    ns, ne, rows_half,
    idt_ref, gt_ref, x_ref, d_ref, wg_hbm, wu_hbm, wd_hbm,
    dt_ref, gg_ref, gu_ref, gd_ref,
    meta_o, meta_i, xin, din, pall, gcol, cx, cd, rx, rd, wgu, wd,
    ab, dh, dd, hid, bi, acc, po, pi, go, gi,
    w_sem, ms, zs, zr, es, er, bs, br, ps, pr, gs, gr,
):
    s = lax.axis_index("seq")
    e = lax.axis_index("exp")
    c = lax.axis_index("edp")
    tok, width = x_ref.shape
    hidn = wd.shape[1]
    half_w = width // 2
    topk = idt_ref.shape[0]
    nch = ns // 2
    rows = 2 * rows_half
    allr = ne * rows
    parts = PARTS
    pw = width // parts
    ct = min(512, pw)
    per = pw // ct

    def span(q):
        return slice(q * pw, (q + 1) * pw)

    def plane(d):
        return (lax.rem(s + d, ns), e, c)

    def plane_back(d):
        return (lax.rem(s + ns - d, ns), e, c)

    def peer_index(j):
        total, bit = 0, 1
        while bit < ne:
            total = total + lax.rem(e // bit + j // bit, 2) * bit
            bit *= 2
        return total

    def peer(j):
        return (s, peer_index(j), c)

    weights = [
        pltpu.make_async_copy(wg_hbm, wgu.at[:, 0:hidn], w_sem.at[0]),
        pltpu.make_async_copy(wu_hbm, wgu.at[:, hidn:2 * hidn], w_sem.at[1]),
        pltpu.make_async_copy(wd_hbm, wd, w_sem.at[2]),
    ]
    for w in weights:
        w.start()

    barrier = pltpu.get_barrier_semaphore()
    for d in range(1, ns):
        pl.semaphore_signal(barrier, inc=1, device_id=plane(d), device_id_type=MESH)
    for j in range(1, ne):
        pl.semaphore_signal(barrier, inc=1, device_id=peer(j), device_id_type=MESH)
    pl.semaphore_signal(barrier, inc=1, device_id=(s, e, 1 - c), device_id_type=MESH)

    experts = ns * ne
    ex = lax.broadcasted_iota(jnp.int32, (experts, tok), 0)
    mask = jnp.zeros((experts, tok), F32)
    gate = jnp.zeros((experts, tok), F32)
    for k in range(topk):
        eq = idt_ref[k:k + 1, :] == ex
        mask = jnp.where(eq, 1.0, mask)
        gate = jnp.where(eq, gt_ref[k:k + 1, :], gate)
    before = (
        lax.broadcasted_iota(jnp.int32, (tok, tok), 0)
        < lax.broadcasted_iota(jnp.int32, (tok, tok), 1)
    )
    rank = jnp.dot(
        mask.astype(BF), jnp.where(before, 1.0, 0.0).astype(BF), preferred_element_type=F32
    )
    slot = jnp.where(mask > 0.0, rank, -4096.0)
    for z in range(ns):
        meta_o[z, 0:ne, :] = slot[z * ne:(z + 1) * ne, :]
        meta_o[z, ne:2 * ne, :] = gate[z * ne:(z + 1) * ne, :]
    meta_i[0] = meta_o[s]

    pl.semaphore_wait(barrier, ns - 1 + ne - 1 + 1)

    def remote(src, dst, ss, rs, dev):
        return pltpu.make_async_remote_copy(
            src_ref=src, dst_ref=dst, send_sem=ss, recv_sem=rs, device_id=dev, device_id_type=MESH
        )

    def grid(*dims):
        if not dims:
            return None
        return [grid(*dims[1:]) for _ in range(dims[0])]

    mcp = grid(ns)
    xcp = grid(ns, parts)
    dcp = grid(ns, parts)
    pout = grid(ns, parts)
    for d in range(1, ns):
        mcp[d] = remote(
            meta_o.at[lax.rem(s + d, ns)], meta_i.at[d], ms.at[0, d], ms.at[1, d], plane(d)
        )
        for q in range(parts):
            cs = span(q)
            xcp[d][q] = remote(
                x_ref.at[:, cs], xin.at[d, :, cs], zs.at[0, d, q], zr.at[0, d, q], plane(d)
            )
            dcp[d][q] = remote(
                d_ref.at[:, cs], din.at[d, :, cs], zs.at[1, d, q], zr.at[1, d, q], plane(d)
            )
            pout[d][q] = remote(
                po.at[d, :, cs], pi.at[d, :, cs], ps.at[d, q], pr.at[d, q], plane_back(d)
            )
    xout = grid(nch, parts, ne)
    dout = grid(nch, parts, ne)
    bout = grid(nch, parts, ne)
    for k in range(nch):
        for q in range(parts):
            cs = span(q)
            for j in range(1, ne):
                at = (k, j, slice(None), cs)
                xout[k][q][j] = remote(
                    cx.at[at], rx.at[at], es.at[0, k, q, j], er.at[0, k, q, j], peer(j)
                )
                dout[k][q][j] = remote(
                    cd.at[at], rd.at[at], es.at[1, k, q, j], er.at[1, k, q, j], peer(j)
                )
                bout[k][q][j] = remote(
                    cx.at[at], bi.at[at], bs.at[k, q, j], br.at[k, q, j], peer(j)
                )
    partner = (s, e, 1 - c)
    gout = [
        remote(go.at[i], gi.at[i], gs.at[i], gr.at[i], partner) for i in range(3)
    ]

    def members(k):
        return (k, k + nch)

    def column(t, size):
        return pl.ds(pl.multiple_of(t * size, size), size)

    def make_select(k):
        da_, db_ = members(k)
        r = lax.broadcasted_iota(jnp.int32, (rows, 2 * tok), 0).astype(F32)
        for j in range(ne):
            idx = peer_index(j)
            sl = jnp.concatenate(
                [
                    meta_i[da_, pl.ds(idx, 1), :],
                    meta_i[db_, pl.ds(idx, 1), :] + float(rows_half),
                ],
                axis=1,
            )
            gl = jnp.concatenate(
                [meta_i[da_, pl.ds(ne + idx, 1), :], meta_i[db_, pl.ds(ne + idx, 1), :]], axis=1
            )
            hit = r == sl
            pall[k, j * rows:(j + 1) * rows, :] = jnp.where(hit, 1.0, 0.0).astype(BF)
            g = jnp.sum(jnp.where(hit, gl, 0.0), axis=1, keepdims=True)
            gcol[j * rows:(j + 1) * rows, :] = jnp.broadcast_to(g, (rows, 128))

    def compact(k, q, own, arrived, out, got, scaled):
        ra, rb = members(k)

        def body(t, carry):
            cs = column(t, ct)
            first = own[:, cs] if ra == 0 else arrived[ra, :, cs]
            both = jnp.concatenate([first, arrived[rb, :, cs]], axis=0)
            y = jnp.dot(pall[k], both, preferred_element_type=F32)
            if scaled:
                y = y * gcol[:, 0:1]
            y = y.astype(BF)
            got[k, 0, :, cs] = y[0:rows]
            for j in range(1, ne):
                out[k, j, :, cs] = y[j * rows:(j + 1) * rows]
            return carry

        lax.fori_loop(q * per, (q + 1) * per, body, 0)

    def gate_up(k):
        for q in range(parts):
            for j in range(1, ne):
                xout[k][q][j].wait_recv()

        def body(t, carry):
            cs = column(t, 256)
            ab[:, cs] = jnp.dot(
                rx[k].reshape(allr, width), wgu[:, cs], preferred_element_type=F32
            )
            return carry

        lax.fori_loop(0, 2 * hidn // 256, body, 0)

    def middle(k):
        for q in range(parts):
            for j in range(1, ne):
                dout[k][q][j].wait_recv()
        dh[...] = jnp.dot(rd[k].reshape(allr, width), wd[...], preferred_element_type=F32)

        def act_body(t, carry):
            rs_ = pl.ds(pl.multiple_of(t * 16, 16), 16)
            a = ab[rs_, 0:hidn]
            b = ab[rs_, hidn:2 * hidn]
            g = dh[rs_, :]
            sig = jax.nn.sigmoid(a)
            act = a * sig
            hid[rs_, :] = (act * b).astype(BF)
            dd[rs_, 0:hidn] = (g * b * sig * (1.0 + a * (1.0 - sig))).astype(BF)
            dd[rs_, hidn:2 * hidn] = (g * act).astype(BF)
            return carry

        lax.fori_loop(0, allr // 16, act_body, 0)
        for q in range(parts):
            for j in range(1, ne):
                xout[k][q][j].wait_send()

        def back_body(t, carry):
            cs = column(t, ct)
            y = lax.dot_general(
                dd[...], wgu[cs, :], (((1,), (1,)), ((), ())), preferred_element_type=F32
            ).astype(BF)
            bi[k, 0, :, cs] = y[0:rows]
            for j in range(1, ne):
                cx[k, j, :, cs] = y[j * rows:(j + 1) * rows]
            return carry

        for q in range(parts):
            lax.fori_loop(q * per, (q + 1) * per, back_body, 0)
            for j in far_first(ne):
                bout[k][q][j].start()

    zero = (((0,), (0,)), ((), ()))

    def grads(k, half, outs):
        gt = min(256, half_w)

        def body(t, carry):
            cs = pl.ds(pl.multiple_of(half * half_w + t * gt, gt), gt)
            rs_ = column(t, gt)
            xt = rx[k, :, :, cs].reshape(allr, gt)
            dt = rd[k, :, :, cs].reshape(allr, gt)
            xg = lax.dot_general(xt, dd[...], zero, preferred_element_type=F32)
            dg = lax.dot_general(dt, hid[...], zero, preferred_element_type=F32)
            if k == 0:
                outs[0][rs_, :] = xg[:, 0:hidn]
                outs[1][rs_, :] = xg[:, hidn:2 * hidn]
                outs[2][rs_, :] = dg
            else:
                outs[0][rs_, :] += xg[:, 0:hidn]
                outs[1][rs_, :] += xg[:, hidn:2 * hidn]
                outs[2][rs_, :] += dg
            return carry

        lax.fori_loop(0, half_w // gt, body, 0)

    def combine(k):
        ra, rb = members(k)

        def body(t, carry):
            cs = column(t, ct)
            y = lax.dot_general(
                pall[k], bi[k, :, :, cs].reshape(allr, ct), zero, preferred_element_type=F32
            )
            if ra == 0:
                acc[:, cs] = y[0:tok]
            else:
                po[ra, :, cs] = y[0:tok].astype(BF)
            po[rb, :, cs] = y[tok:2 * tok].astype(BF)
            return carry

        for q in range(parts):
            for j in range(1, ne):
                bout[k][q][j].wait_recv()
            lax.fori_loop(q * per, (q + 1) * per, body, 0)
            for d in (rb, ra):
                if d:
                    pout[d][q].start()

    def arrive(copies, k, q):
        for d in members(k):
            if d:
                copies[d][q].wait_recv()

    def depart(copies, k):
        for q in range(parts):
            for d in members(k):
                if d:
                    copies[d][q].start()

    def arrive_meta(k):
        for d in members(k):
            if d:
                mcp[d].wait_recv()

    for d in range(1, ns):
        mcp[d].start()
    depart(xcp, 0)
    depart(dcp, 0)
    arrive_meta(0)
    make_select(0)
    for k in range(nch):
        if k:
            arrive_meta(k)
            make_select(k)
        for q in range(parts):
            arrive(xcp, k, q)
            compact(k, q, x_ref, xin, cx, rx, False)
            for j in far_first(ne):
                xout[k][q][j].start()
        if k + 1 < nch:
            depart(xcp, k + 1)
            depart(dcp, k + 1)
        if k:
            middle(k - 1)
        for q in range(parts):
            arrive(dcp, k, q)
            compact(k, q, d_ref, din, cd, rd, True)
            for j in far_first(ne):
                dout[k][q][j].start()
        if k == 0:
            for w in weights:
                w.wait()
        else:
            grads(k - 1, 1 - c, (go.at[0], go.at[1], go.at[2]))
            grads(k - 1, c, (gg_ref, gu_ref, gd_ref))
            combine(k - 1)
        gate_up(k)
    last = nch - 1
    middle(last)
    grads(last, 1 - c, (go.at[0], go.at[1], go.at[2]))
    for g in gout:
        g.start()
    grads(last, c, (gg_ref, gu_ref, gd_ref))
    combine(last)
    for g in gout:
        g.wait_recv()
    gg_ref[...] += gi[0]
    gu_ref[...] += gi[1]
    gd_ref[...] += gi[2]

    def final(t, carry):
        cs = column(t, ct)
        y = acc[:, cs]
        for d in range(1, ns):
            y = y + pi[d, :, cs].astype(F32)
        dt_ref[:, cs] = y.astype(BF)
        return carry

    for q in range(parts):
        for d in range(1, ns):
            pout[d][q].wait_recv()
        lax.fori_loop(q * per, (q + 1) * per, final, 0)
    for d in range(1, ns):
        mcp[d].wait_send()
        for q in range(parts):
            xcp[d][q].wait_send()
            dcp[d][q].wait_send()
            pout[d][q].wait_send()
    for k in range(nch):
        for q in range(parts):
            for j in range(1, ne):
                dout[k][q][j].wait_send()
                bout[k][q][j].wait_send()
    for g in gout:
        g.wait_send()


def sizes(ns, ne, tok, topk, width, hidn):
    experts = ns * ne
    capacity = tok * topk // experts + max(1, tok * topk // (8 * experts))
    rows_half = -(-capacity // 8) * 8
    rows = 2 * rows_half
    nch = max(1, ns // 2)
    allr = ne * rows
    scratch = [
        ((ns, 2 * ne, tok), F32),
        ((ns, 2 * ne, tok), F32),
        ((ns, tok, width), BF),
        ((ns, tok, width), BF),
        ((nch, allr, 2 * tok), BF),
        ((allr, 128), F32),
        ((nch, ne, rows, width), BF),
        ((nch, ne, rows, width), BF),
        ((nch, ne, rows, width), BF),
        ((nch, ne, rows, width), BF),
        ((width, 2 * hidn), BF),
        ((width, hidn), BF),
        ((allr, 2 * hidn), F32),
        ((allr, hidn), F32),
        ((allr, 2 * hidn), BF),
        ((allr, hidn), BF),
        ((nch, ne, rows, width), BF),
        ((tok, width), F32),
        ((ns, tok, width), BF),
        ((ns, tok, width), BF),
        ((3, width // 2, hidn), F32),
        ((3, width // 2, hidn), F32),
    ]
    total = 0
    for shape, kind in scratch:
        n = 1
        for v in shape:
            n *= v
        total += n * jnp.dtype(kind).itemsize
    total += 3 * (width // 2) * hidn * 4 + 3 * tok * width * 2
    return rows_half, nch, scratch, total


def fused(tokens, route_ids, gates, d_out, w_gate, w_up, w_down):
    ns = lax.axis_size("seq")
    ne = lax.axis_size("exp")
    tok, width = tokens.shape
    topk = route_ids.shape[1]
    hidn = w_gate.shape[2]
    rows_half, nch, scratch, _ = sizes(ns, ne, tok, topk, width, hidn)
    dma = pltpu.SemaphoreType.DMA
    vm = pl.BlockSpec(memory_space=pltpu.VMEM)
    hbm = pl.BlockSpec(memory_space=pl.ANY)
    half = jax.ShapeDtypeStruct((width // 2, hidn), F32)
    pairs = tok * ns * topk * 9 // 8
    out = pl.pallas_call(
        functools.partial(fused_kernel, ns, ne, rows_half),
        out_shape=(jax.ShapeDtypeStruct((tok, width), BF), half, half, half),
        in_specs=[vm, vm, vm, vm, hbm, hbm, hbm],
        out_specs=(vm, vm, vm, vm),
        scratch_shapes=[pltpu.VMEM(sh, kind) for sh, kind in scratch] + [
            dma((3,)),
            dma((2, ns)),
            dma((2, ns, PARTS)), dma((2, ns, PARTS)),
            dma((2, nch, PARTS, ne)), dma((2, nch, PARTS, ne)),
            dma((nch, PARTS, ne)), dma((nch, PARTS, ne)),
            dma((ns, PARTS)), dma((ns, PARTS)),
            dma((3,)), dma((3,)),
        ],
        compiler_params=pltpu.CompilerParams(
            collective_id=0, has_side_effects=True, vmem_limit_bytes=VMEM_BYTES
        ),
        cost_estimate=pl.CostEstimate(
            flops=16 * pairs * width * hidn, bytes_accessed=12 * width * hidn, transcendentals=0
        ),
    )(route_ids.T, gates.T, tokens, d_out, w_gate[0], w_up[0], w_down[0])
    return (out[0], out[1][None], out[2][None], out[3][None])


def solution(mesh):
    in_specs = (
        P(("seq", "exp", "edp"), None),
        P(("seq", "exp", "edp"), None),
        P(("seq", "exp", "edp"), None),
        P(("seq", "exp", "edp"), None),
        P(("seq", "exp"), None, None),
        P(("seq", "exp"), None, None),
        P(("seq", "exp"), None, None),
    )
    out_specs = (
        P(("seq", "exp", "edp"), None),
        P(("seq", "exp"), "edp", None),
        P(("seq", "exp"), "edp", None),
        P(("seq", "exp"), "edp", None),
    )
    def shard(body):
        return jax.shard_map(
            body, mesh=mesh, in_specs=in_specs, out_specs=out_specs, check_vma=False
        )

    ns, ne, nd = mesh.shape["seq"], mesh.shape["exp"], mesh.shape["edp"]

    def whole(tokens, route_ids, gates, d_out, w_gate, w_up, w_down):
        tok = tokens.shape[0] // (ns * ne * nd)
        total = sizes(ns, ne, tok, route_ids.shape[1], tokens.shape[1], w_gate.shape[2])[3]
        fits = total < VMEM_BYTES - 3 * 1024 * 1024
        body = fused if fits and ns % 2 == 0 and nd == 2 and ne & (ne - 1) == 0 and tok % 128 == 0 else on_device
        return shard(body)(tokens, route_ids, gates, d_out, w_gate, w_up, w_down)

    return whole
```
